128 devices in a mesh: blk: 128 (over z, x, y, core).
Axes of the slice: x: 4, y: 4, z: 4, core: 2. Of those that a mesh axis runs over, the one named last changes fastest.
Arguments:
- fitted_tensor: bfloat16 [384, 3, 256, 2048], P('blk'), may hold values from -0.125 to 0.125
- block_slot: int32 [256], replicated, may hold values from 0 to 383, as said below
- pair_list: int32 [6144, 2], replicated, may hold values from 0 to 255, as said below
- domain_slots: int32 [6144, 4], replicated, may hold values from 0 to 2
Outputs:
- exchange: float32 [384, 256, 256], P('blk')
The draws below stay inside these ranges and needn't reach their ends.
Inputs may be any that keep to these rules, and one draw needn't show every extreme that they name: `block_slot`: slots rise with block numbers. The blocks owned by device d fill its first slots d * 3, d * 3 + 1, ...; every device owns 1 to 3 blocks, devices 2j and 2j + 1 own 2 * 2 together, and some device owns 3. `pair_list`: each row (a, b) has a < b <= a + 2; some row reaches b = a + 2 with the owners 2 devices apart.
All inputs are finite; a program needn't handle non-finite values.
Results may differ from the reference program's by a relative error of at most 0.0003.
Values may be sent and summed in bfloat16 or wider, within the bound.
No kernel may reach another device: no remote copies, remote signals or barrier semaphores. Data moves between devices by JAX's collectives and lax.ppermute only.
A program may use at most 256 MiB of HBM per device.

```python
import jax
import jax.numpy as jnp
from jax import lax

BS = 256
LOC = 3
ND = 2
REACH = 2
BLK_DEV = 2
OWN_CAP = 3
X = 2048
NBLK = 256
SLOTS = 384
PAIRS = 6144


def draw_block_slot(key, part):
    key = jax.random.fold_in(key, 11)
    pair_count = NBLK // (2 * BLK_DEV)
    shares = jax.random.randint(key, (pair_count,), 1, OWN_CAP + 1)
    shares = shares.at[0].set(OWN_CAP)
    owned = jnp.stack([shares, 2 * BLK_DEV - shares], axis=1).reshape(-1)
    devices = jnp.repeat(jnp.arange(owned.shape[0]), owned, total_repeat_length=NBLK)
    starts = jnp.cumsum(owned) - owned
    position = jnp.arange(NBLK) - starts[devices]
    return (devices * OWN_CAP + position).astype(jnp.int32)


def draw_pair_list(key, part):
    key = jax.random.fold_in(key, 23)
    first_key, step_key = jax.random.split(key)
    steps = jax.random.randint(step_key, (PAIRS,), 1, REACH + 1)
    starts = jax.random.randint(first_key, (PAIRS,), 0, NBLK - REACH)
    starts = starts.at[0].set(OWN_CAP - 1)
    steps = steps.at[0].set(REACH)
    return jnp.stack([starts, starts + steps], axis=1).astype(jnp.int32)


def plant(drawn, key, low, high):
    longest = drawn.shape.index(max(drawn.shape))
    spots = []
    for shift in (0, 1):
        where = [jax.random.randint(jax.random.fold_in(key, axis), (), 0, length) for axis, length in enumerate(drawn.shape)]
        where[longest] = (where[longest] + shift) % drawn.shape[longest]
        spots.append(tuple(where))
    return drawn.at[spots[0]].set(low).at[spots[1]].set(high)


def level_of(own_key, shape, cuts, least, largest):
    factor_of = 1.0
    for dim, blocks in cuts:
        heights = jax.random.uniform(jax.random.fold_in(jax.random.fold_in(own_key, 6), dim), (blocks,), jnp.float32, least / len(cuts), largest / len(cuts))
        factor_of = factor_of * jnp.repeat(jnp.exp(heights), shape[dim] // blocks).reshape((-1,) + (1,) * (len(shape) - 1 - dim))
    return factor_of


def noise(stream_key, dims, width, reach, pieces=(), kind=jnp.bfloat16):
    loudness = level_of(stream_key, dims, pieces, -0.22, 0.18) if pieces else 1.0
    entries = jax.random.normal(stream_key, dims, jnp.float32) * width * loudness
    return jnp.minimum(jnp.maximum(entries, -reach), reach).astype(kind)


def setup_inputs(seed: int = 0) -> dict:
    key_list = jax.random.split(jax.random.key(seed), 5)
    return {
        "fitted_tensor": noise(key_list[0], (SLOTS, LOC, BS, X), X ** -0.5, 0.125, ((0, 128),)),
        "block_slot": draw_block_slot(jax.random.fold_in(key_list[4], 71), 0),
        "pair_list": draw_pair_list(jax.random.fold_in(key_list[4], 71), 0),
        "domain_slots": plant(jax.random.randint(key_list[3], (PAIRS, 2 * ND), 0, LOC), jax.random.fold_in(key_list[3], 1), 0, LOC - 1).astype(jnp.int32),
    }


def merged_rows(block_rows):
    return jnp.transpose(block_rows, (1, 0, 2)).reshape(block_rows.shape[1], -1)


def reference(fitted_tensor, block_slot, pair_list, domain_slots):
    def diag_one(slot_index):
        flat_rows = merged_rows(fitted_tensor[slot_index])
        return jnp.dot(flat_rows, flat_rows.T, preferred_element_type=jnp.float32)

    diagonal = lax.map(diag_one, block_slot)
    exchange = jnp.zeros((fitted_tensor.shape[0], BS, BS), jnp.float32)
    exchange = exchange.at[block_slot].set(diagonal)

    def one_pair(exchange_sum, item):
        pair_row, domain_row = item
        slot_first = block_slot[pair_row[0]]
        slot_second = block_slot[pair_row[1]]
        left_rows = merged_rows(fitted_tensor[slot_first][domain_row[:ND]])
        right_rows = merged_rows(fitted_tensor[slot_second][domain_row[ND:]])
        pair_block = jnp.dot(left_rows, right_rows.T, preferred_element_type=jnp.float32)
        exchange_sum = exchange_sum.at[slot_first].add(pair_block)
        exchange_sum = exchange_sum.at[slot_second].add(pair_block.T)
        return exchange_sum, None

    exchange, unused = lax.scan(one_pair, exchange, (pair_list, domain_slots))
    return exchange
```

```python
import functools

import jax
import jax.numpy as jnp
from jax import lax
from jax.experimental import pallas as pl
from jax.experimental.pallas import tpu as pltpu
from jax.sharding import PartitionSpec as P

CHUNKS = (1536, 512)
MIB = 1024 * 1024
MAIN_LIMIT, EARLY_LIMIT, LATE_LIMIT = 20 * MIB, 12 * MIB, 12 * MIB
F32 = jnp.float32


def dot_rows(left, right):
    return lax.dot_general(left, right, (((1,), (1,)), ((), ())), preferred_element_type=F32)


def flat(block):
    return block.reshape(block.shape[0] * block.shape[1], block.shape[2])


def layout(cap, me, slots_ref):
    even = me % 2 == 0
    start = me // 2 * 4
    odd_live = slots_ref[start + 3] % cap + 1
    live = jnp.where(even, 4 - odd_live, odd_live)
    return live, jnp.where(even, start, start + 4 - odd_live), even


def in_hbm(value):
    return pltpu.with_memory_space_constraint(value, pltpu.HBM)


def pick_kernel(cap, spans, me_ref, slots_ref, own_ref, *refs):
    outs, sems = refs[:-1], refs[-1]
    live, _, even = layout(cap, me_ref[0], slots_ref)
    slot = jnp.where(even, 0, live - 1)
    copies = []
    for n, (start, size) in enumerate(spans):
        for k in range(3):
            copies.append(
                pltpu.make_async_copy(
                    own_ref.at[slot, k, :, pl.ds(start, size)], outs[n].at[k], sems.at[n, k]
                )
            )
    for copy in copies:
        copy.start()
    for copy in copies:
        copy.wait()


def pick(me, block_slot, own, spans):
    cap, aux, rows, _ = own.shape
    hbm = pl.BlockSpec(memory_space=pltpu.HBM)
    moved = sum(size for _, size in spans) * aux * rows * 4
    return pl.pallas_call(
        functools.partial(pick_kernel, cap, spans),
        out_shape=tuple(jax.ShapeDtypeStruct((aux, rows, size), own.dtype) for _, size in spans),
        in_specs=[
            pl.BlockSpec(memory_space=pltpu.SMEM),
            pl.BlockSpec(memory_space=pltpu.SMEM),
            hbm,
        ],
        out_specs=(pl.BlockSpec(memory_space=pltpu.VMEM),) * len(spans),
        scratch_shapes=[pltpu.SemaphoreType.DMA((len(spans), aux))],
        name="pick",
        cost_estimate=pl.CostEstimate(flops=0, bytes_accessed=moved, transcendentals=0),
    )(me.reshape(1), block_slot, in_hbm(own))


def counts_kernel(cap, me_ref, slots_ref, pairs_ref, domain_ref, counts_ref, meta_ref):
    live, first, even = layout(cap, me_ref[0], slots_ref)
    meta_ref[0] = live
    meta_ref[1] = even.astype(jnp.int32)
    meta_ref[2] = jnp.where(even, 0, live - 1)
    meta_ref[3] = jnp.where(live == 1, 0, jnp.where(even, 1, live - 2))
    meta_ref[4] = jnp.where(even, live - 1, 0)
    meta_ref[5] = jnp.where(live == 1, 0, jnp.where(even, live - 2, 1))
    meta_ref[6] = jnp.where(even, 0, cap - live)
    meta_ref[7] = 0
    a = pairs_ref[0:1, :]
    b = pairs_ref[1:2, :]
    edge = (a - (first - 1)) * 2 + (b - a - 1)
    size = a.shape[1]
    rows = lax.broadcasted_iota(jnp.int32, (16, size), 0)
    hot = jnp.where(rows == edge, 1.0, 0.0).astype(jnp.bfloat16)
    weight = jnp.zeros((16, size), F32)
    for j in range(2):
        code = domain_ref[j : j + 1, :] * 3 + domain_ref[j + 2 : j + 3, :]
        weight = weight + jnp.where(rows == code, 1.0, 0.0)
    counts_ref[...] = dot_rows(hot, weight.astype(jnp.bfloat16))


def pair_counts(me, block_slot, pair_list, domain_slots, cap):
    pairs, domain = pair_list.T, domain_slots.T
    vmem = pl.BlockSpec(memory_space=pltpu.VMEM)
    smem = pl.BlockSpec(memory_space=pltpu.SMEM)
    return pl.pallas_call(
        functools.partial(counts_kernel, cap),
        out_shape=(jax.ShapeDtypeStruct((16, 16), F32), jax.ShapeDtypeStruct((8,), jnp.int32)),
        in_specs=[smem, smem, vmem, vmem],
        out_specs=(vmem, smem),
        name="pair_counts",
        cost_estimate=pl.CostEstimate(flops=4_000_000, bytes_accessed=200_000, transcendentals=0),
    )(me.reshape(1), block_slot, pairs, domain)


def weigh(counts_ref, row, step_left, step_right, left, right_of, total_ref):
    rows = left.shape[0] // 3

    for l in range(3):
        product = dot_rows(left, right_of(l))
        total = total_ref[...]
        for k in range(3):
            count = counts_ref[row, k * step_left + l * step_right]
            total = total + count * product[k * rows : (k + 1) * rows]
        total_ref[...] = total


def split(counts_ref, row, step_own, step_halo, aux_of, l):
    total = None
    for k in range(3):
        part = counts_ref[row, k * step_own + l * step_halo] * aux_of(k).astype(F32)
        total = part if total is None else total + part
    high = total.astype(jnp.bfloat16)
    return high, (total - high.astype(F32)).astype(jnp.bfloat16)


def main_kernel(
    meta_ref, counts_ref, own_hbm, partner_hbm, sum_ref, back_ref, mix_early, mix_late, own_ref, inner_ref, edge_ref, sems
):
    live, even = meta_ref[0], meta_ref[1] == 1
    adj_out, sec_out, adjacent, second = meta_ref[2], meta_ref[3], meta_ref[4], meta_ref[5]
    adj_mine = (live == 1) | ((live == 2) & even)
    step_own = jnp.where(even, 3, 1)
    step_halo = jnp.where(even, 1, 3)
    rows = own_ref.shape[2]

    def own_copy(s):
        return pltpu.make_async_copy(own_hbm.at[s], own_ref.at[s], sems.at[s])

    inner_copy = pltpu.make_async_copy(partner_hbm.at[meta_ref[6]], inner_ref, sems.at[3])
    for s in range(3):
        own_copy(s).start()
    inner_copy.start()
    back_ref[...] = jnp.zeros_like(back_ref)
    def diag(s, carry):
        own_copy(s).wait()

        @pl.when(s < live)
        def _():
            total = dot_rows(own_ref[s, 0], own_ref[s, 0])
            for k in range(1, 3):
                total = total + dot_rows(own_ref[s, k], own_ref[s, k])
            sum_ref[s] = total

        @pl.when(s >= live)
        def _():
            sum_ref[s] = jnp.zeros((rows, rows), F32)

        return carry

    lax.fori_loop(0, 3, diag, 0)

    def own_edge(e, carry):
        i, j = e // 2, jnp.minimum(e + 1, 2)

        @pl.when(j < live)
        def _():
            row = (i + 1) * 2 + (j - i - 1)
            edge_ref[...] = jnp.zeros_like(edge_ref)
            weigh(counts_ref, row, 3, 1, flat(own_ref[i]), lambda l: own_ref[j, l], edge_ref)
            sum_ref[i] += edge_ref[...]
            sum_ref[j] += edge_ref[...].T

        return carry

    lax.fori_loop(0, 3, own_edge, 0)

    inner_copy.wait()

    def put(e, row, source):
        def one(n, carry):
            l, r = n // (rows // 32), pl.multiple_of(n % (rows // 32) * 32, 32)
            high, low = split(counts_ref, row, step_halo, step_own, lambda k: source(k, r), l)
            early = mix_early.shape[-1]
            for part, values in ((0, high), (1, low)):
                where = pl.ds((2 * e + part) * rows + r, 32)
                mix_early[l, where] = values[:, :early]
                mix_late[l, where] = values[:, early:]
            return carry

        lax.fori_loop(0, 3 * rows // 32, one, 0)

    row_adj = jnp.where(even, 0, live * 2)
    row_sec = jnp.where(even, 1, (live - 1) * 2 + 1)
    put(0, row_adj, lambda k, r: own_ref[adj_out, k, pl.ds(r, 32)])

    @pl.when(live >= 2)
    def _():
        put(1, row_sec, lambda k, r: own_ref[sec_out, k, pl.ds(r, 32)])

    @pl.when(live == 1)
    def _():
        put(1, row_sec, lambda k, r: inner_ref[k, pl.ds(r, 32)])

    def inner_edge(e, carry):
        slot = jnp.where(e == 0, adjacent, second)

        @pl.when(jnp.where(e == 0, adj_mine, live >= 2))
        def _():
            row = jnp.where(even, jnp.where(e == 0, live * 2, (live - 1) * 2 + 1), e)
            edge_ref[...] = jnp.zeros_like(edge_ref)
            weigh(
                counts_ref, row, step_own, step_halo, flat(own_ref[slot]), lambda l: inner_ref[l], edge_ref
            )
            sum_ref[slot] += edge_ref[...]
            back_ref[...] += edge_ref[...].T

        return carry

    lax.fori_loop(0, 2, inner_edge, 0)


def main_part(meta, counts, own, partner):
    cap, aux, rows, width = own.shape
    smem = pl.BlockSpec(memory_space=pltpu.SMEM)
    vmem = pl.BlockSpec(memory_space=pltpu.VMEM)
    hbm = pl.BlockSpec(memory_space=pltpu.HBM)
    return pl.pallas_call(
        main_kernel,
        in_specs=[smem, smem, hbm, pl.BlockSpec(memory_space=pl.ANY)],
        out_specs=(vmem, vmem, vmem, vmem),
        scratch_shapes=[
            pltpu.VMEM((cap, aux, rows, width), own.dtype),
            pltpu.VMEM((aux, rows, width), own.dtype),
            pltpu.VMEM((rows, rows), F32),
            pltpu.SemaphoreType.DMA((4,)),
        ],
        out_shape=(
            jax.ShapeDtypeStruct((cap, rows, rows), F32),
            jax.ShapeDtypeStruct((rows, rows), F32),
            pltpu.VMEM((aux, 4 * rows, CHUNKS[0]), own.dtype),
            pltpu.VMEM((aux, 4 * rows, CHUNKS[1]), own.dtype),
        ),
        compiler_params=pltpu.CompilerParams(vmem_limit_bytes=MAIN_LIMIT),
        name="own_and_inner",
        cost_estimate=pl.CostEstimate(
            flops=60 * 2 * rows * rows * width, bytes_accessed=26_000_000, transcendentals=0
        ),
    )(meta, counts, in_hbm(own), partner)


def mixed(mix_ref, outer_ref):
    total = None
    for l in range(3):
        part = dot_rows(mix_ref[l], outer_ref[l])
        total = part if total is None else total + part
    rows = total.shape[0] // 4
    return total[:rows] + total[rows : 2 * rows], total[2 * rows : 3 * rows] + total[3 * rows :]


def early_kernel(mix_ref, outer_ref, adj_ref, sec_ref):
    adj_ref[...], sec_ref[...] = mixed(mix_ref, outer_ref)


def early_part(mix, outer):
    aux, rows, width = outer.shape
    vmem = pl.BlockSpec(memory_space=pltpu.VMEM)
    return pl.pallas_call(
        early_kernel,
        in_specs=[vmem] * 2,
        out_specs=(vmem,) * 2,
        out_shape=(jax.ShapeDtypeStruct((rows, rows), F32),) * 2,
        compiler_params=pltpu.CompilerParams(vmem_limit_bytes=EARLY_LIMIT),
        name="outer_early",
        cost_estimate=pl.CostEstimate(
            flops=12 * 2 * rows * rows * width, bytes_accessed=1_000_000, transcendentals=0
        ),
    )(mix, outer)


def late_kernel(meta_ref, mix_ref, outer_ref, adj_in, sec_in, inner_in, back_ref, inner_ref, adj_ref, sec_ref):
    adj, sec = mixed(mix_ref, outer_ref)
    sec = sec_in[...] + sec
    back_ref[...] = sec.T
    sec_ref[...] = sec
    inner_ref[...] = inner_in[...] + jnp.where(meta_ref[0] == 1, sec, 0.0)
    adj_ref[...] = adj_in[...] + adj


def late_part(meta, mix, outer, adj, sec, inner_back):
    aux, rows, width = outer.shape
    square = jax.ShapeDtypeStruct((rows, rows), F32)
    vmem = pl.BlockSpec(memory_space=pltpu.VMEM)
    return pl.pallas_call(
        late_kernel,
        in_specs=[pl.BlockSpec(memory_space=pltpu.SMEM)] + [vmem] * 5,
        out_specs=(vmem,) * 4,
        out_shape=(square,) * 4,
        compiler_params=pltpu.CompilerParams(vmem_limit_bytes=LATE_LIMIT),
        name="outer_late",
        cost_estimate=pl.CostEstimate(
            flops=12 * 2 * rows * rows * width, bytes_accessed=6_000_000, transcendentals=0
        ),
    )(meta, mix, outer, adj, sec, inner_back)


def settle_kernel(meta_ref, sum_ref, adj_ref, sec_ref, out_ref):
    out_ref[...] = sum_ref[...]
    out_ref[meta_ref[2]] += adj_ref[...]

    @pl.when(meta_ref[0] >= 2)
    def _():
        out_ref[meta_ref[3]] += sec_ref[...]


def finish_kernel(meta_ref, sum_ref, outer_ref, inner_ref, out_ref):
    out_ref[...] = sum_ref[...]
    out_ref[meta_ref[2]] += outer_ref[...]
    out_ref[meta_ref[4]] += inner_ref[...]


def add_blocks(kernel, name, meta, total, first, second):
    vmem = pl.BlockSpec(memory_space=pltpu.VMEM)
    return pl.pallas_call(
        kernel,
        in_specs=[pl.BlockSpec(memory_space=pltpu.SMEM)] + [vmem] * 3,
        out_specs=vmem,
        out_shape=jax.ShapeDtypeStruct(total.shape, F32),
        compiler_params=pltpu.CompilerParams(vmem_limit_bytes=LATE_LIMIT),
        name=name,
        cost_estimate=pl.CostEstimate(flops=200_000, bytes_accessed=2_000_000, transcendentals=0),
    )(meta, total, first, second)


def per_device(own, block_slot, pair_list, domain_slots):
    cap = own.shape[0]
    count = lax.axis_size("blk")
    me = lax.axis_index("blk")
    to_outer = [(d, d - 1) for d in range(2, count, 2)] + [(d, d + 1) for d in range(1, count - 1, 2)]
    to_inner = [(d, d ^ 1) for d in range(count)]
    first, late = CHUNKS
    (early_piece,) = pick(me, block_slot, own, [(0, first)])
    outer_early = lax.ppermute(early_piece, "blk", to_outer)
    (late_piece,) = pick(me, block_slot, own, [(first, late)])
    outer_late = lax.ppermute(late_piece, "blk", to_outer)
    partner = lax.ppermute(own, "blk", to_inner)
    counts, meta = pair_counts(me, block_slot, pair_list, domain_slots, cap)
    own_sum, inner_back, mix_early, mix_late = main_part(meta, counts, own, partner)
    adj, sec = early_part(mix_early, outer_early)
    outer_back, inner_back, adj, sec = late_part(meta, mix_late, outer_late, adj, sec, inner_back)
    from_outer = lax.ppermute(outer_back, "blk", to_outer)
    from_inner = lax.ppermute(inner_back, "blk", to_inner)
    total = add_blocks(settle_kernel, "settle", meta, own_sum, adj, sec)
    return add_blocks(finish_kernel, "finish", meta, total, from_outer, from_inner)


def solution(mesh):
    placed = (P("blk", None, None, None), P(), P(), P())
    return jax.shard_map(
        per_device, mesh=mesh, in_specs=placed, out_specs=P("blk", None, None), check_vma=False
    )
```

```python
import functools

import jax
import jax.numpy as jnp
from jax import lax
from jax.experimental import pallas as pl
from jax.experimental.pallas import tpu as pltpu
from jax.sharding import PartitionSpec as P

EARLY = 1792
MIB = 1024 * 1024
MAIN_LIMIT, EARLY_LIMIT, LATE_LIMIT = 24 * MIB, 12 * MIB, 12 * MIB
F32 = jnp.float32
BLOCK = 256
TOKEN = pltpu.VMEM((8, 128), jnp.float32)


def dot_rows(left, right):
    return lax.dot_general(left, right, (((1,), (1,)), ((), ())), preferred_element_type=F32)


def flat(block):
    return block.reshape(block.shape[0] * block.shape[1], block.shape[2])


def layout(cap, me, slots_ref):
    even = me % 2 == 0
    start = me // 2 * 4
    odd_live = slots_ref[start + 3] % cap + 1
    live = jnp.where(even, 4 - odd_live, odd_live)
    return live, jnp.where(even, start, start + 4 - odd_live), even


def in_hbm(value):
    return pltpu.with_memory_space_constraint(value, pltpu.HBM)


def run_copies(pairs, sems):
    copies = [pltpu.make_async_copy(source, target, sems.at[n]) for n, (source, target) in enumerate(pairs)]
    for copy in copies:
        copy.start()
    for copy in copies:
        copy.wait()


def pick_kernel(cap, me_ref, slots_ref, own_ref, out_ref, sems):
    live, _, even = layout(cap, me_ref[0], slots_ref)
    slot = jnp.where(even, 0, live - 1)
    width = out_ref.shape[-1]
    part = own_ref.shape[2] // 4
    run_copies(
        [
            (
                own_ref.at[slot, k, pl.ds(q * part, part), pl.ds(0, width)],
                out_ref.at[k, pl.ds(q * part, part)],
            )
            for k in range(3)
            for q in range(4)
        ],
        sems,
    )


def pick_two_kernel(cap, start, me_ref, slots_ref, own_ref, partner_ref, after, out_ref, token_ref, sems):
    del after
    token_ref[...] = jnp.zeros_like(token_ref)
    live, _, even = layout(cap, me_ref[0], slots_ref)
    width = out_ref.shape[-1]
    columns = pl.ds(start, width)
    slot = jnp.where(even, 0, live - 1)
    first = [(own_ref.at[slot, k, :, columns], out_ref.at[0, k]) for k in range(3)]

    @pl.when(live >= 2)
    def _():
        second = jnp.where(even, 1, live - 2)
        run_copies(first + [(own_ref.at[second, k, :, columns], out_ref.at[1, k]) for k in range(3)], sems)

    @pl.when(live == 1)
    def _():
        second = jnp.where(even, 0, cap - live)
        run_copies(first + [(partner_ref.at[second, k, :, columns], out_ref.at[1, k]) for k in range(3)], sems)


def pick_call(kernel, name, shape, me, block_slot, blocks, *after):
    smem = pl.BlockSpec(memory_space=pltpu.SMEM)
    moved = 4
    for size in shape:
        moved *= size
    return pl.pallas_call(
        kernel,
        out_shape=(pltpu.VMEM(shape, blocks[0].dtype),) + (TOKEN,) * (len(blocks) - 1),
        in_specs=[smem, smem, pl.BlockSpec(memory_space=pltpu.HBM)]
        + [pl.BlockSpec(memory_space=pl.ANY)] * (len(blocks) - 1 + len(after)),
        out_specs=(pl.BlockSpec(memory_space=pltpu.VMEM),) * len(blocks),
        scratch_shapes=[pltpu.SemaphoreType.DMA((12,))],
        compiler_params=pltpu.CompilerParams(vmem_limit_bytes=LATE_LIMIT),
        name=name,
        cost_estimate=pl.CostEstimate(flops=0, bytes_accessed=moved, transcendentals=0),
    )(me.reshape(1), in_hbm(block_slot), in_hbm(blocks[0]), *blocks[1:], *after)


def pick_early(me, block_slot, own):
    cap, aux, rows, _ = own.shape
    return pick_call(
        functools.partial(pick_kernel, cap), "pick", (aux, rows, EARLY), me, block_slot, [own]
    )[0]


def pick_late(me, block_slot, own, partner, after):
    cap, aux, rows, width = own.shape
    return pick_call(
        functools.partial(pick_two_kernel, cap, EARLY),
        "pick_two",
        (2, aux, rows, width - EARLY),
        me,
        block_slot,
        [own, partner],
        after,
    )


def counts_kernel(cap, me_ref, slots_ref, pairs_ref, domain_ref, counts_ref, meta_ref):
    live, first, even = layout(cap, me_ref[0], slots_ref)
    values = (
        live,
        even.astype(jnp.int32),
        jnp.where(even, 0, live - 1),
        jnp.where(live == 1, 0, jnp.where(even, 1, live - 2)),
        jnp.where(even, live - 1, 0),
        jnp.where(live == 1, 0, jnp.where(even, live - 2, 1)),
        jnp.where(even, 0, cap - live),
    )
    lanes = lax.broadcasted_iota(jnp.int32, meta_ref.shape, 1)
    meta = jnp.zeros(meta_ref.shape, jnp.int32)
    for n, value in enumerate(values):
        meta = jnp.where(lanes == n, value, meta)
    meta_ref[...] = meta
    a = pairs_ref[0:1, :]
    b = pairs_ref[1:2, :]
    edge = (a - (first - 2)) * 2 + (b - a - 1)
    size = a.shape[1]
    rows = lax.broadcasted_iota(jnp.int32, (16, size), 0)
    hot = jnp.where(rows == edge, 1.0, 0.0).astype(jnp.bfloat16)
    weight = jnp.zeros((16, size), F32)
    for j in range(2):
        code = domain_ref[j : j + 1, :] * 3 + domain_ref[j + 2 : j + 3, :]
        weight = weight + jnp.where(rows == code, 1.0, 0.0)
    counts_ref[...] = dot_rows(hot, weight.astype(jnp.bfloat16))


def pair_counts(me, block_slot, pair_list, domain_slots, cap):
    pairs, domain = pair_list.T, domain_slots.T
    vmem = pl.BlockSpec(memory_space=pltpu.VMEM)
    smem = pl.BlockSpec(memory_space=pltpu.SMEM)
    return pl.pallas_call(
        functools.partial(counts_kernel, cap),
        out_shape=(pltpu.VMEM((16, 16), F32), pltpu.VMEM((8, 128), jnp.int32)),
        in_specs=[smem, smem, vmem, vmem],
        out_specs=(vmem, vmem),
        compiler_params=pltpu.CompilerParams(vmem_limit_bytes=LATE_LIMIT),
        name="pair_counts",
        cost_estimate=pl.CostEstimate(flops=4_000_000, bytes_accessed=200_000, transcendentals=0),
    )(me.reshape(1), block_slot, pairs, domain)


def weigh(counts_ref, row, step_left, step_right, left, right_of, total_ref):
    rows = left.shape[0] // 3

    for l in range(3):
        product = dot_rows(left, right_of(l))
        total = total_ref[...]
        for k in range(3):
            count = counts_ref[row, k * step_left + l * step_right]
            total = total + count * product[k * rows : (k + 1) * rows]
        total_ref[...] = total


def split(counts_ref, row, step_own, step_halo, aux_of, l):
    total = None
    for k in range(3):
        part = counts_ref[row, k * step_own + l * step_halo] * aux_of(k).astype(F32)
        total = part if total is None else total + part
    high = total.astype(jnp.bfloat16)
    return high, (total - high.astype(F32)).astype(jnp.bfloat16)


def fill(counts_ref, row, step_own, step_halo, source, store):
    rows = BLOCK

    def one(n, carry):
        l, r = n // (rows // 32), pl.multiple_of(n % (rows // 32) * 32, 32)
        high, low = split(counts_ref, row, step_own, step_halo, lambda k: source(k, r), l)
        store(l, r, high)
        store(l, rows + r, low)
        return carry

    lax.fori_loop(0, 3 * rows // 32, one, 0)


def store_columns(early, early_ref, late_ref):
    def store(l, r, values):
        early_ref[l, pl.ds(r, 32)] = values[:, :early]
        late_ref[l, pl.ds(r, 32)] = values[:, early:]

    return store


def edge_kernel(meta_ref, counts_ref, own_hbm, mix_early, mix_late, mix_far, own_ref, sem):
    live, even = meta_ref[0, 0], meta_ref[0, 1] == 1
    copy = pltpu.make_async_copy(own_hbm.at[meta_ref[0, 2]], own_ref, sem)
    copy.start()
    step_own = jnp.where(even, 1, 3)
    step_halo = jnp.where(even, 3, 1)
    early = mix_early.shape[-1]
    copy.wait()

    def far_store(l, r, values):
        mix_far[l, pl.ds(r, 32)] = values

    row_adj = jnp.where(even, 2, live * 2 + 2)
    row_far = jnp.where(even, 1, live * 2 + 3)
    store = store_columns(early, mix_early, mix_late)
    fill(counts_ref, row_adj, step_own, step_halo, lambda k, r: own_ref[k, pl.ds(r, 32)], store)
    fill(counts_ref, row_far, step_own, step_halo, lambda k, r: own_ref[k, pl.ds(r, 32), early:], far_store)


def edge_part(meta, counts, own):
    cap, aux, rows, width = own.shape
    late = width - EARLY
    smem = pl.BlockSpec(memory_space=pltpu.SMEM)
    vmem = pl.BlockSpec(memory_space=pltpu.VMEM)
    return pl.pallas_call(
        edge_kernel,
        in_specs=[smem, smem, pl.BlockSpec(memory_space=pltpu.HBM)],
        out_specs=(vmem,) * 3,
        scratch_shapes=[pltpu.VMEM((aux, rows, width), own.dtype), pltpu.SemaphoreType.DMA(())],
        out_shape=tuple(pltpu.VMEM((aux, 2 * rows, size), own.dtype) for size in (EARLY, late, late)),
        compiler_params=pltpu.CompilerParams(vmem_limit_bytes=EARLY_LIMIT),
        name="edge_mix",
        cost_estimate=pl.CostEstimate(flops=30_000_000, bytes_accessed=10_000_000, transcendentals=0),
    )(meta, counts, in_hbm(own))


def main_kernel(
    meta_ref, counts_ref, own_hbm, partner_hbm, after, sum_ref, back_ref, mix_early, mix_late,
    own_ref, inner_ref, edge_ref, sems
):
    del after
    live, even = meta_ref[0, 0], meta_ref[0, 1] == 1
    sec_out, adjacent, second = meta_ref[0, 3], meta_ref[0, 4], meta_ref[0, 5]
    step_own = jnp.where(even, 3, 1)
    step_halo = jnp.where(even, 1, 3)
    _, _, rows, width = own_ref.shape

    def own_copy(s):
        return pltpu.make_async_copy(own_hbm.at[s], own_ref.at[s], sems.at[s])

    inner_copy = pltpu.make_async_copy(partner_hbm.at[meta_ref[0, 6]], inner_ref.at[0], sems.at[3])
    second_copy = pltpu.make_async_copy(partner_hbm.at[1], inner_ref.at[1], sems.at[4])
    for s in range(3):
        pl.when(s < live)(own_copy(s).start)
        if s == 0:
            pl.when(live < 3)(inner_copy.start)
            pl.when(live == 1)(second_copy.start)
    back_ref[...] = jnp.zeros_like(back_ref)

    def diag(s, carry):
        @pl.when(s < live)
        def _():
            own_copy(s).wait()
            total = dot_rows(own_ref[s, 0], own_ref[s, 0])
            for k in range(1, 3):
                total = total + dot_rows(own_ref[s, k], own_ref[s, k])
            sum_ref[s] = total

        @pl.when(s >= live)
        def _():
            sum_ref[s] = jnp.zeros((rows, rows), F32)

        return carry

    lax.fori_loop(0, 3, diag, 0)

    def own_edge(e, carry):
        i, j = e // 2, jnp.minimum(e + 1, 2)
        theirs = (live == 3) & (e == jnp.where(even, 2, 0))

        @pl.when((j < live) & jnp.logical_not(theirs))
        def _():
            row = (i + 2) * 2 + (j - i - 1)
            edge_ref[...] = jnp.zeros_like(edge_ref)
            weigh(counts_ref, row, 3, 1, flat(own_ref[i]), lambda l: own_ref[j, l], edge_ref)
            sum_ref[i] += edge_ref[...]
            sum_ref[j] += edge_ref[...].T

        return carry

    lax.fori_loop(0, 3, own_edge, 0)
    pl.when(live < 3)(inner_copy.wait)
    pl.when(live == 1)(second_copy.wait)
    half = width // 2

    def inner_edge(t, carry):
        e, side = t // 2, t % 2
        mine = (live == 1) | ((live == 2) & ((e == 1) | (side == jnp.where(even, 0, 1))))

        @pl.when(mine)
        def _():
            slot = jnp.where(e == 0, adjacent, second)
            halo = jnp.where((live == 1) & (e == 1), 1, 0)
            row_one = jnp.where(live == 1, jnp.where(even, 5, 1), jnp.where(even, live * 2 + 1, 3))
            row = jnp.where(e == 0, jnp.where(even, live * 2 + 2, 2), row_one)
            columns = pl.ds(pl.multiple_of(side * half, half), half)
            edge_ref[...] = jnp.zeros_like(edge_ref)
            weigh(
                counts_ref,
                row,
                step_own,
                step_halo,
                flat(own_ref[slot, :, :, columns]),
                lambda l: inner_ref[halo, l, :, columns],
                edge_ref,
            )
            sum_ref[slot] += edge_ref[...]
            back_ref[halo] += edge_ref[...].T

        return carry

    lax.fori_loop(0, 4, inner_edge, 0)

    @pl.when(live == 1)
    def _():
        row = jnp.where(even, 6, 0)
        edge_ref[...] = jnp.zeros_like(edge_ref)
        weigh(counts_ref, row, step_own, step_halo, flat(inner_ref[0]), lambda l: inner_ref[1, l], edge_ref)
        back_ref[0] += edge_ref[...]
        back_ref[1] += edge_ref[...].T

    early = mix_early.shape[-1]

    def put(source):
        row = jnp.where(even, 3, live * 2 + 1)
        fill(counts_ref, row, step_halo, step_own, source, store_columns(early, mix_early, mix_late))

    pl.when(live >= 2)(lambda: put(lambda k, r: own_ref[sec_out, k, pl.ds(r, 32)]))
    pl.when(live == 1)(lambda: put(lambda k, r: inner_ref[0, k, pl.ds(r, 32)]))


def main_part(meta, counts, own, partner, after):
    cap, aux, rows, width = own.shape
    late = width - EARLY
    smem = pl.BlockSpec(memory_space=pltpu.SMEM)
    vmem = pl.BlockSpec(memory_space=pltpu.VMEM)
    hbm = pl.BlockSpec(memory_space=pltpu.HBM)
    free = pl.BlockSpec(memory_space=pl.ANY)
    return pl.pallas_call(
        main_kernel,
        in_specs=[smem, smem, hbm, free, free],
        out_specs=(vmem,) * 4,
        scratch_shapes=[
            pltpu.VMEM((cap, aux, rows, width), own.dtype),
            pltpu.VMEM((2, aux, rows, width), own.dtype),
            pltpu.VMEM((rows, rows), F32),
            pltpu.SemaphoreType.DMA((5,)),
        ],
        out_shape=(
            jax.ShapeDtypeStruct((cap, rows, rows), F32),
            jax.ShapeDtypeStruct((2, rows, rows), F32),
            pltpu.VMEM((aux, 2 * rows, EARLY), own.dtype),
            pltpu.VMEM((aux, 2 * rows, late), own.dtype),
        ),
        compiler_params=pltpu.CompilerParams(vmem_limit_bytes=MAIN_LIMIT),
        name="own_and_inner",
        cost_estimate=pl.CostEstimate(
            flops=50 * 2 * rows * rows * width, bytes_accessed=16_000_000, transcendentals=0
        ),
    )(meta, counts, in_hbm(own), partner, after)


def mixed(mix_ref, right_of):
    total = None
    for l in range(3):
        part = dot_rows(mix_ref[l], right_of(l))
        total = part if total is None else total + part
    rows = total.shape[1]
    return total[:rows] + total[rows:]


def early_kernel(mix_ref, outer_ref, back_ref, sec_ref):
    sec = mixed(mix_ref, lambda l: outer_ref[l])
    back_ref[...] = sec.T
    sec_ref[...] = sec


def early_part(mix, outer):
    aux, rows, width = outer.shape
    vmem = pl.BlockSpec(memory_space=pltpu.VMEM)
    return pl.pallas_call(
        early_kernel,
        in_specs=[vmem] * 2,
        out_specs=(vmem,) * 2,
        out_shape=(jax.ShapeDtypeStruct((rows, rows), F32),) * 2,
        compiler_params=pltpu.CompilerParams(vmem_limit_bytes=EARLY_LIMIT),
        name="outer_early",
        cost_estimate=pl.CostEstimate(
            flops=6 * 2 * rows * rows * width, bytes_accessed=1_000_000, transcendentals=0
        ),
    )(mix, outer)


def adjacent_kernel(mix_ref, outer_ref, adj_ref):
    adj_ref[...] = mixed(mix_ref, lambda l: outer_ref[l])


def adjacent_part(mix, outer):
    aux, rows, width = outer.shape
    vmem = pl.BlockSpec(memory_space=pltpu.VMEM)
    return pl.pallas_call(
        adjacent_kernel,
        in_specs=[vmem] * 2,
        out_specs=vmem,
        out_shape=jax.ShapeDtypeStruct((rows, rows), F32),
        compiler_params=pltpu.CompilerParams(vmem_limit_bytes=EARLY_LIMIT),
        name="outer_adjacent",
        cost_estimate=pl.CostEstimate(
            flops=6 * 2 * rows * rows * width, bytes_accessed=1_000_000, transcendentals=0
        ),
    )(mix, outer)


def late_kernel(
    meta_ref, adj_mix, sec_mix, far_mix, outer_ref, adj_in, sec_in, inner_in, adj_ref, sec_ref, *inner_refs
):
    sec = sec_in[...] + mixed(sec_mix, lambda l: outer_ref[0, l])
    adj = mixed(adj_mix, lambda l: outer_ref[0, l]) + mixed(far_mix, lambda l: outer_ref[1, l])
    near = inner_in[0] + jnp.where(meta_ref[0, 0] == 1, sec, 0.0)
    half = near.shape[0] // 2
    inner_refs[0][...] = near[:half]
    inner_refs[1][...] = near[half:]
    inner_refs[2][...] = inner_in[1, :half]
    inner_refs[3][...] = inner_in[1, half:]
    sec_ref[...] = sec
    adj_ref[...] = adj_in[...] + adj


def late_part(meta, mixes, outer, adj, sec, inner_back):
    _, aux, rows, width = outer.shape
    square = jax.ShapeDtypeStruct((rows, rows), F32)
    vmem = pl.BlockSpec(memory_space=pltpu.VMEM)
    return pl.pallas_call(
        late_kernel,
        in_specs=[pl.BlockSpec(memory_space=pltpu.SMEM)] + [vmem] * 7,
        out_specs=(vmem,) * 6,
        out_shape=(square, square) + (jax.ShapeDtypeStruct((rows // 2, rows), F32),) * 4,
        compiler_params=pltpu.CompilerParams(vmem_limit_bytes=LATE_LIMIT),
        name="outer_late",
        cost_estimate=pl.CostEstimate(
            flops=18 * 2 * rows * rows * width, bytes_accessed=1_000_000, transcendentals=0
        ),
    )(meta, *mixes, outer, adj, sec, inner_back)


def settle_kernel(meta_ref, sum_ref, adj_ref, sec_ref, out_ref):
    out_ref[...] = sum_ref[...]
    out_ref[meta_ref[0, 2]] += adj_ref[...]

    @pl.when(meta_ref[0, 0] >= 2)
    def _():
        out_ref[meta_ref[0, 3]] += sec_ref[...]


def finish_kernel(meta_ref, sum_ref, outer_ref, near_top, near_low, next_top, next_low, out_ref):
    out_ref[...] = sum_ref[...]
    out_ref[meta_ref[0, 2]] += outer_ref[...]
    half = near_top.shape[0]
    out_ref[meta_ref[0, 4], :half] += near_top[...]
    out_ref[meta_ref[0, 4], half:] += near_low[...]
    out_ref[meta_ref[0, 5], :half] += next_top[...]
    out_ref[meta_ref[0, 5], half:] += next_low[...]


def add_blocks(kernel, name, meta, total, *blocks):
    vmem = pl.BlockSpec(memory_space=pltpu.VMEM)
    return pl.pallas_call(
        kernel,
        in_specs=[pl.BlockSpec(memory_space=pltpu.SMEM)] + [vmem] * (1 + len(blocks)),
        out_specs=vmem,
        out_shape=jax.ShapeDtypeStruct(total.shape, F32),
        compiler_params=pltpu.CompilerParams(vmem_limit_bytes=LATE_LIMIT),
        name=name,
        cost_estimate=pl.CostEstimate(flops=200_000, bytes_accessed=2_000_000, transcendentals=0),
    )(meta, total, *blocks)


def per_device(own, block_slot, pair_list, domain_slots):
    cap = own.shape[0]
    count = lax.axis_size("blk")
    me = lax.axis_index("blk")
    to_outer = [(d, d - 1) for d in range(2, count, 2)] + [(d, d + 1) for d in range(1, count - 1, 2)]
    to_inner = [(d, d ^ 1) for d in range(count)]
    outer_early = lax.ppermute(pick_early(me, block_slot, own), "blk", to_outer)
    partner = lax.ppermute(own, "blk", to_inner)
    counts, meta = pair_counts(me, block_slot, pair_list, domain_slots, cap)
    adj_early, adj_late, mix_far = edge_part(meta, counts, own)
    late_piece, token = pick_late(me, block_slot, own, partner, mix_far)
    outer_late = lax.ppermute(late_piece, "blk", to_outer)
    own_sum, inner_back, sec_early, sec_late = main_part(meta, counts, own, partner, token)
    outer_back, sec = early_part(sec_early, outer_early)
    from_outer = lax.ppermute(outer_back, "blk", to_outer)
    adj = adjacent_part(adj_early, outer_early)
    adj, sec, *backs = late_part(meta, (adj_late, sec_late, mix_far), outer_late, adj, sec, inner_back)
    from_inner = [lax.ppermute(piece, "blk", to_inner) for piece in backs]
    total = add_blocks(settle_kernel, "settle", meta, own_sum, adj, sec)
    return add_blocks(finish_kernel, "finish", meta, total, from_outer, *from_inner)


def solution(mesh):
    placed = (P("blk", None, None, None), P(), P(), P())
    return jax.shard_map(
        per_device, mesh=mesh, in_specs=placed, out_specs=P("blk", None, None), check_vma=False
    )
```

```python
import functools

import jax
import jax.numpy as jnp
from jax import lax
from jax.experimental import pallas as pl
from jax.experimental.pallas import tpu as pltpu
from jax.sharding import PartitionSpec as P

EARLY = 1792
MIB = 1024 * 1024
MAIN_LIMIT, EARLY_LIMIT, LATE_LIMIT = 24 * MIB, 12 * MIB, 12 * MIB
F32 = jnp.float32
BLOCK = 256
TOKEN = pltpu.VMEM((8, 128), jnp.float32)


def dot_rows(left, right):
    return lax.dot_general(left, right, (((1,), (1,)), ((), ())), preferred_element_type=F32)


def flat(block):
    return block.reshape(block.shape[0] * block.shape[1], block.shape[2])


def layout(cap, me, slots_ref):
    even = me % 2 == 0
    start = me // 2 * 4
    odd_live = slots_ref[start + 3] % cap + 1
    live = jnp.where(even, 4 - odd_live, odd_live)
    return live, jnp.where(even, start, start + 4 - odd_live), even


def in_hbm(value):
    return pltpu.with_memory_space_constraint(value, pltpu.HBM)


def run_copies(pairs, sems):
    copies = [pltpu.make_async_copy(source, target, sems.at[n]) for n, (source, target) in enumerate(pairs)]
    for copy in copies:
        copy.start()
    for copy in copies:
        copy.wait()


def pick_kernel(cap, me_ref, slots_ref, own_ref, out_ref, sems):
    live, _, even = layout(cap, me_ref[0], slots_ref)
    slot = jnp.where(even, 0, live - 1)
    width = out_ref.shape[-1]
    part = own_ref.shape[2] // 4
    run_copies(
        [
            (
                own_ref.at[slot, k, pl.ds(q * part, part), pl.ds(0, width)],
                out_ref.at[k, pl.ds(q * part, part)],
            )
            for k in range(3)
            for q in range(4)
        ],
        sems,
    )


def pick_two_kernel(cap, start, me_ref, slots_ref, own_ref, partner_ref, after, out_ref, token_ref, sems):
    del after
    token_ref[...] = jnp.zeros_like(token_ref)
    live, _, even = layout(cap, me_ref[0], slots_ref)
    width = out_ref.shape[-1]
    columns = pl.ds(start, width)
    slot = jnp.where(even, 0, live - 1)
    first = [(own_ref.at[slot, k, :, columns], out_ref.at[0, k]) for k in range(3)]

    @pl.when(live >= 2)
    def _():
        second = jnp.where(even, 1, live - 2)
        run_copies(first + [(own_ref.at[second, k, :, columns], out_ref.at[1, k]) for k in range(3)], sems)

    @pl.when(live == 1)
    def _():
        second = jnp.where(even, 0, cap - live)
        run_copies(first + [(partner_ref.at[second, k, :, columns], out_ref.at[1, k]) for k in range(3)], sems)


def pick_call(kernel, name, shape, me, block_slot, blocks, *after):
    smem = pl.BlockSpec(memory_space=pltpu.SMEM)
    moved = 4
    for size in shape:
        moved *= size
    return pl.pallas_call(
        kernel,
        out_shape=(pltpu.VMEM(shape, blocks[0].dtype),) + (TOKEN,) * (len(blocks) - 1),
        in_specs=[smem, smem, pl.BlockSpec(memory_space=pltpu.HBM)]
        + [pl.BlockSpec(memory_space=pl.ANY)] * (len(blocks) - 1 + len(after)),
        out_specs=(pl.BlockSpec(memory_space=pltpu.VMEM),) * len(blocks),
        scratch_shapes=[pltpu.SemaphoreType.DMA((12,))],
        compiler_params=pltpu.CompilerParams(vmem_limit_bytes=LATE_LIMIT),
        name=name,
        cost_estimate=pl.CostEstimate(flops=0, bytes_accessed=moved, transcendentals=0),
    )(me.reshape(1), in_hbm(block_slot), in_hbm(blocks[0]), *blocks[1:], *after)


def pick_early(me, block_slot, own):
    cap, aux, rows, _ = own.shape
    return pick_call(
        functools.partial(pick_kernel, cap), "pick", (aux, rows, EARLY), me, block_slot, [own]
    )[0]


def pick_late(me, block_slot, own, partner, after):
    cap, aux, rows, width = own.shape
    return pick_call(
        functools.partial(pick_two_kernel, cap, EARLY),
        "pick_two",
        (2, aux, rows, width - EARLY),
        me,
        block_slot,
        [own, partner],
        after,
    )


def counts_kernel(cap, me_ref, slots_ref, pairs_ref, domain_ref, counts_ref, meta_ref):
    live, first, even = layout(cap, me_ref[0], slots_ref)
    values = (
        live,
        even.astype(jnp.int32),
        jnp.where(even, 0, live - 1),
        jnp.where(live == 1, 0, jnp.where(even, 1, live - 2)),
        jnp.where(even, live - 1, 0),
        jnp.where(live == 1, 0, jnp.where(even, live - 2, 1)),
        jnp.where(even, 0, cap - live),
    )
    lanes = lax.broadcasted_iota(jnp.int32, meta_ref.shape, 1)
    meta = jnp.zeros(meta_ref.shape, jnp.int32)
    for n, value in enumerate(values):
        meta = jnp.where(lanes == n, value, meta)
    meta_ref[...] = meta
    a = pairs_ref[0:1, :]
    b = pairs_ref[1:2, :]
    edge = (a - (first - 2)) * 2 + (b - a - 1)
    size = a.shape[1]
    rows = lax.broadcasted_iota(jnp.int32, (16, size), 0)
    hot = jnp.where(rows == edge, 1.0, 0.0).astype(jnp.bfloat16)
    weight = jnp.zeros((16, size), F32)
    for j in range(2):
        code = domain_ref[j : j + 1, :] * 3 + domain_ref[j + 2 : j + 3, :]
        weight = weight + jnp.where(rows == code, 1.0, 0.0)
    counts_ref[...] = dot_rows(hot, weight.astype(jnp.bfloat16))


def pair_counts(me, block_slot, pair_list, domain_slots, cap):
    pairs, domain = pair_list.T, domain_slots.T
    vmem = pl.BlockSpec(memory_space=pltpu.VMEM)
    smem = pl.BlockSpec(memory_space=pltpu.SMEM)
    return pl.pallas_call(
        functools.partial(counts_kernel, cap),
        out_shape=(pltpu.VMEM((16, 16), F32), pltpu.VMEM((8, 128), jnp.int32)),
        in_specs=[smem, smem, vmem, vmem],
        out_specs=(vmem, vmem),
        compiler_params=pltpu.CompilerParams(vmem_limit_bytes=LATE_LIMIT),
        name="pair_counts",
        cost_estimate=pl.CostEstimate(flops=4_000_000, bytes_accessed=200_000, transcendentals=0),
    )(me.reshape(1), block_slot, pairs, domain)


def weigh(counts_ref, row, step_left, step_right, left, right_of, total_ref):
    rows = left.shape[0] // 3

    for l in range(3):
        product = dot_rows(left, right_of(l))
        total = total_ref[...]
        for k in range(3):
            count = counts_ref[row, k * step_left + l * step_right]
            total = total + count * product[k * rows : (k + 1) * rows]
        total_ref[...] = total


def split(counts_ref, row, step_own, step_halo, aux_of, l):
    total = None
    for k in range(3):
        part = counts_ref[row, k * step_own + l * step_halo] * aux_of(k).astype(F32)
        total = part if total is None else total + part
    high = total.astype(jnp.bfloat16)
    return high, (total - high.astype(F32)).astype(jnp.bfloat16)


def fill(counts_ref, row, step_own, step_halo, source, store):
    rows = BLOCK

    def one(n, carry):
        l, r = n // (rows // 32), pl.multiple_of(n % (rows // 32) * 32, 32)
        high, low = split(counts_ref, row, step_own, step_halo, lambda k: source(k, r), l)
        store(l, r, high)
        store(l, rows + r, low)
        return carry

    lax.fori_loop(0, 3 * rows // 32, one, 0)


def store_columns(early, early_ref, late_ref):
    def store(l, r, values):
        early_ref[l, pl.ds(r, 32)] = values[:, :early]
        late_ref[l, pl.ds(r, 32)] = values[:, early:]

    return store


def edge_kernel(meta_ref, counts_ref, own_hbm, mix_early, mix_late, mix_far, own_ref, sem):
    live, even = meta_ref[0, 0], meta_ref[0, 1] == 1
    copy = pltpu.make_async_copy(own_hbm.at[meta_ref[0, 2]], own_ref, sem)
    copy.start()
    step_own = jnp.where(even, 1, 3)
    step_halo = jnp.where(even, 3, 1)
    early = mix_early.shape[-1]
    copy.wait()

    def far_store(l, r, values):
        mix_far[l, pl.ds(r, 32)] = values

    row_adj = jnp.where(even, 2, live * 2 + 2)
    row_far = jnp.where(even, 1, live * 2 + 3)
    store = store_columns(early, mix_early, mix_late)
    fill(counts_ref, row_adj, step_own, step_halo, lambda k, r: own_ref[k, pl.ds(r, 32)], store)
    fill(counts_ref, row_far, step_own, step_halo, lambda k, r: own_ref[k, pl.ds(r, 32), early:], far_store)


def edge_part(meta, counts, own):
    cap, aux, rows, width = own.shape
    late = width - EARLY
    smem = pl.BlockSpec(memory_space=pltpu.SMEM)
    vmem = pl.BlockSpec(memory_space=pltpu.VMEM)
    return pl.pallas_call(
        edge_kernel,
        in_specs=[smem, smem, pl.BlockSpec(memory_space=pltpu.HBM)],
        out_specs=(vmem,) * 3,
        scratch_shapes=[pltpu.VMEM((aux, rows, width), own.dtype), pltpu.SemaphoreType.DMA(())],
        out_shape=tuple(pltpu.VMEM((aux, 2 * rows, size), own.dtype) for size in (EARLY, late, late)),
        compiler_params=pltpu.CompilerParams(vmem_limit_bytes=EARLY_LIMIT),
        name="edge_mix",
        cost_estimate=pl.CostEstimate(flops=30_000_000, bytes_accessed=10_000_000, transcendentals=0),
    )(meta, counts, in_hbm(own))


def main_kernel(
    meta_ref, counts_ref, own_hbm, partner_hbm, after, sum_ref, near_ref, next_ref, mix_early, mix_late,
    own_ref, inner_ref, edge_ref, sems
):
    del after
    live, even = meta_ref[0, 0], meta_ref[0, 1] == 1
    sec_out, adjacent, second = meta_ref[0, 3], meta_ref[0, 4], meta_ref[0, 5]
    step_own = jnp.where(even, 3, 1)
    step_halo = jnp.where(even, 1, 3)
    _, _, rows, width = own_ref.shape

    def own_copy(s):
        return pltpu.make_async_copy(own_hbm.at[s], own_ref.at[s], sems.at[s])

    inner_copy = pltpu.make_async_copy(partner_hbm.at[meta_ref[0, 6]], inner_ref.at[0], sems.at[3])
    second_copy = pltpu.make_async_copy(partner_hbm.at[1], inner_ref.at[1], sems.at[4])
    for s in range(3):
        pl.when(s < live)(own_copy(s).start)
        if s == 0:
            pl.when(live < 3)(inner_copy.start)
            pl.when(live == 1)(second_copy.start)
    near_ref[...] = jnp.zeros_like(near_ref)
    next_ref[...] = jnp.zeros_like(next_ref)

    def diag(s, carry):
        @pl.when(s < live)
        def _():
            own_copy(s).wait()
            total = dot_rows(own_ref[s, 0], own_ref[s, 0])
            for k in range(1, 3):
                total = total + dot_rows(own_ref[s, k], own_ref[s, k])
            sum_ref[s] = total

        @pl.when(s >= live)
        def _():
            sum_ref[s] = jnp.zeros((rows, rows), F32)

        return carry

    lax.fori_loop(0, 3, diag, 0)

    def own_edge(e, carry):
        i, j = e // 2, jnp.minimum(e + 1, 2)
        theirs = (live == 3) & (e == jnp.where(even, 2, 0))

        @pl.when((j < live) & jnp.logical_not(theirs))
        def _():
            row = (i + 2) * 2 + (j - i - 1)
            edge_ref[...] = jnp.zeros_like(edge_ref)
            weigh(counts_ref, row, 3, 1, flat(own_ref[i]), lambda l: own_ref[j, l], edge_ref)
            sum_ref[i] += edge_ref[...]
            sum_ref[j] += edge_ref[...].T

        return carry

    lax.fori_loop(0, 3, own_edge, 0)
    pl.when(live < 3)(inner_copy.wait)
    pl.when(live == 1)(second_copy.wait)
    half = width // 2

    def inner_edge(t, carry):
        e, side = t // 2, t % 2
        mine = (live == 1) | ((live == 2) & ((e == 1) | (side == jnp.where(even, 0, 1))))

        @pl.when(mine)
        def _():
            slot = jnp.where(e == 0, adjacent, second)
            halo = jnp.where((live == 1) & (e == 1), 1, 0)
            row_one = jnp.where(live == 1, jnp.where(even, 5, 1), jnp.where(even, live * 2 + 1, 3))
            row = jnp.where(e == 0, jnp.where(even, live * 2 + 2, 2), row_one)
            columns = pl.ds(pl.multiple_of(side * half, half), half)
            edge_ref[...] = jnp.zeros_like(edge_ref)
            weigh(
                counts_ref,
                row,
                step_own,
                step_halo,
                flat(own_ref[slot, :, :, columns]),
                lambda l: inner_ref[halo, l, :, columns],
                edge_ref,
            )
            sum_ref[slot] += edge_ref[...]

            @pl.when(halo == 0)
            def _():
                near_ref[...] += edge_ref[...].T

            @pl.when(halo == 1)
            def _():
                next_ref[...] += edge_ref[...].T


        return carry

    lax.fori_loop(0, 4, inner_edge, 0)

    @pl.when(live == 1)
    def _():
        row = jnp.where(even, 6, 0)
        edge_ref[...] = jnp.zeros_like(edge_ref)
        weigh(counts_ref, row, step_own, step_halo, flat(inner_ref[0]), lambda l: inner_ref[1, l], edge_ref)
        near_ref[...] += edge_ref[...]
        next_ref[...] += edge_ref[...].T

    early = mix_early.shape[-1]

    def put(source):
        row = jnp.where(even, 3, live * 2 + 1)
        fill(counts_ref, row, step_halo, step_own, source, store_columns(early, mix_early, mix_late))

    pl.when(live >= 2)(lambda: put(lambda k, r: own_ref[sec_out, k, pl.ds(r, 32)]))
    pl.when(live == 1)(lambda: put(lambda k, r: inner_ref[0, k, pl.ds(r, 32)]))


def main_part(meta, counts, own, partner, after):
    cap, aux, rows, width = own.shape
    late = width - EARLY
    smem = pl.BlockSpec(memory_space=pltpu.SMEM)
    vmem = pl.BlockSpec(memory_space=pltpu.VMEM)
    hbm = pl.BlockSpec(memory_space=pltpu.HBM)
    free = pl.BlockSpec(memory_space=pl.ANY)
    return pl.pallas_call(
        main_kernel,
        in_specs=[smem, smem, hbm, free, free],
        out_specs=(vmem,) * 5,
        scratch_shapes=[
            pltpu.VMEM((cap, aux, rows, width), own.dtype),
            pltpu.VMEM((2, aux, rows, width), own.dtype),
            pltpu.VMEM((rows, rows), F32),
            pltpu.SemaphoreType.DMA((5,)),
        ],
        out_shape=(
            jax.ShapeDtypeStruct((cap, rows, rows), F32),
            jax.ShapeDtypeStruct((rows, rows), F32),
            jax.ShapeDtypeStruct((rows, rows), F32),
            pltpu.VMEM((aux, 2 * rows, EARLY), own.dtype),
            pltpu.VMEM((aux, 2 * rows, late), own.dtype),
        ),
        compiler_params=pltpu.CompilerParams(vmem_limit_bytes=MAIN_LIMIT),
        name="own_and_inner",
        cost_estimate=pl.CostEstimate(
            flops=50 * 2 * rows * rows * width, bytes_accessed=16_000_000, transcendentals=0
        ),
    )(meta, counts, in_hbm(own), partner, after)


def mixed(mix_ref, right_of):
    total = None
    for l in range(3):
        part = dot_rows(mix_ref[l], right_of(l))
        total = part if total is None else total + part
    rows = total.shape[1]
    return total[:rows] + total[rows:]


def early_kernel(mix_ref, outer_ref, back_ref, sec_ref):
    sec = mixed(mix_ref, lambda l: outer_ref[l])
    back_ref[...] = sec.T
    sec_ref[...] = sec


def early_part(mix, outer):
    aux, rows, width = outer.shape
    vmem = pl.BlockSpec(memory_space=pltpu.VMEM)
    return pl.pallas_call(
        early_kernel,
        in_specs=[vmem] * 2,
        out_specs=(vmem,) * 2,
        out_shape=(jax.ShapeDtypeStruct((rows, rows), F32),) * 2,
        compiler_params=pltpu.CompilerParams(vmem_limit_bytes=EARLY_LIMIT),
        name="outer_early",
        cost_estimate=pl.CostEstimate(
            flops=6 * 2 * rows * rows * width, bytes_accessed=1_000_000, transcendentals=0
        ),
    )(mix, outer)


def adjacent_kernel(mix_ref, outer_ref, adj_ref):
    adj_ref[...] = mixed(mix_ref, lambda l: outer_ref[l])


def adjacent_part(mix, outer):
    aux, rows, width = outer.shape
    vmem = pl.BlockSpec(memory_space=pltpu.VMEM)
    return pl.pallas_call(
        adjacent_kernel,
        in_specs=[vmem] * 2,
        out_specs=vmem,
        out_shape=jax.ShapeDtypeStruct((rows, rows), F32),
        compiler_params=pltpu.CompilerParams(vmem_limit_bytes=EARLY_LIMIT),
        name="outer_adjacent",
        cost_estimate=pl.CostEstimate(
            flops=6 * 2 * rows * rows * width, bytes_accessed=1_000_000, transcendentals=0
        ),
    )(mix, outer)


def late_kernel(
    meta_ref, adj_mix, sec_mix, far_mix, outer_ref, adj_in, sec_in, inner_in, adj_ref, sec_ref, *inner_refs
):
    sec = sec_in[...] + mixed(sec_mix, lambda l: outer_ref[0, l])
    adj = mixed(adj_mix, lambda l: outer_ref[0, l]) + mixed(far_mix, lambda l: outer_ref[1, l])
    near = inner_in[...] + jnp.where(meta_ref[0, 0] == 1, sec, 0.0)
    half = near.shape[0] // 2
    inner_refs[0][...] = near[:half]
    inner_refs[1][...] = near[half:]
    sec_ref[...] = sec
    adj_ref[...] = adj_in[...] + adj


def late_part(meta, mixes, outer, adj, sec, inner_back):
    _, aux, rows, width = outer.shape
    square = jax.ShapeDtypeStruct((rows, rows), F32)
    vmem = pl.BlockSpec(memory_space=pltpu.VMEM)
    return pl.pallas_call(
        late_kernel,
        in_specs=[pl.BlockSpec(memory_space=pltpu.SMEM)] + [vmem] * 7,
        out_specs=(vmem,) * 4,
        out_shape=(square, square) + (jax.ShapeDtypeStruct((rows // 2, rows), F32),) * 2,
        compiler_params=pltpu.CompilerParams(vmem_limit_bytes=LATE_LIMIT),
        name="outer_late",
        cost_estimate=pl.CostEstimate(
            flops=18 * 2 * rows * rows * width, bytes_accessed=1_000_000, transcendentals=0
        ),
    )(meta, *mixes, outer, adj, sec, inner_back)


def settle_kernel(meta_ref, sum_ref, adj_ref, sec_ref, next_ref, out_ref, place_ref):
    out_ref[...] = sum_ref[...]
    out_ref[meta_ref[0, 5]] += next_ref[...]
    out_ref[meta_ref[0, 2]] += adj_ref[...]

    @pl.when(meta_ref[0, 0] >= 2)
    def _():
        out_ref[meta_ref[0, 3]] += sec_ref[...]

    row = lax.broadcasted_iota(jnp.int32, place_ref.shape, 0)
    hit = (row == meta_ref[0, 2]) | (row == meta_ref[0, 4] + 3)
    place_ref[...] = jnp.where(hit, 1.0, 0.0)


def settle(meta, total, *blocks):
    vmem = pl.BlockSpec(memory_space=pltpu.VMEM)
    return pl.pallas_call(
        settle_kernel,
        in_specs=[pl.BlockSpec(memory_space=pltpu.SMEM)] + [vmem] * (1 + len(blocks)),
        out_specs=(vmem, vmem),
        out_shape=(pltpu.VMEM(total.shape, F32), pltpu.VMEM((8, total.shape[2]), F32)),
        compiler_params=pltpu.CompilerParams(vmem_limit_bytes=LATE_LIMIT),
        name="settle",
        cost_estimate=pl.CostEstimate(flops=200_000, bytes_accessed=2_000_000, transcendentals=0),
    )(meta, total, *blocks)


def finish_kernel(place_ref, sum_ref, outer_ref, near_top, near_low, out_ref):
    half = near_top.shape[0]
    for s in range(3):
        for rows, near in ((slice(0, half), near_top), (slice(half, 2 * half), near_low)):
            out_ref[s, rows] = (
                sum_ref[s, rows]
                + place_ref[s : s + 1] * outer_ref[rows]
                + place_ref[3 + s : 4 + s] * near[...]
            )


def finish(place, total, *blocks):
    vmem = pl.BlockSpec(memory_space=pltpu.VMEM)
    return pl.pallas_call(
        finish_kernel,
        in_specs=[vmem] * (2 + len(blocks)),
        out_specs=vmem,
        out_shape=jax.ShapeDtypeStruct(total.shape, F32),
        compiler_params=pltpu.CompilerParams(vmem_limit_bytes=LATE_LIMIT),
        name="finish",
        cost_estimate=pl.CostEstimate(flops=200_000, bytes_accessed=2_000_000, transcendentals=0),
    )(place, total, *blocks)


def per_device(own, block_slot, pair_list, domain_slots):
    cap = own.shape[0]
    count = lax.axis_size("blk")
    me = lax.axis_index("blk")
    to_outer = [(d, d - 1) for d in range(2, count, 2)] + [(d, d + 1) for d in range(1, count - 1, 2)]
    to_inner = [(d, d ^ 1) for d in range(count)]
    outer_early = lax.ppermute(pick_early(me, block_slot, own), "blk", to_outer)
    partner = lax.ppermute(own, "blk", to_inner)
    counts, meta = pair_counts(me, block_slot, pair_list, domain_slots, cap)
    adj_early, adj_late, mix_far = edge_part(meta, counts, own)
    late_piece, token = pick_late(me, block_slot, own, partner, mix_far)
    outer_late = lax.ppermute(late_piece, "blk", to_outer)
    own_sum, inner_back, next_back, sec_early, sec_late = main_part(meta, counts, own, partner, token)
    from_next = lax.ppermute(next_back, "blk", to_inner)
    outer_back, sec = early_part(sec_early, outer_early)
    from_outer = lax.ppermute(outer_back, "blk", to_outer)
    adj = adjacent_part(adj_early, outer_early)
    adj, sec, *backs = late_part(meta, (adj_late, sec_late, mix_far), outer_late, adj, sec, inner_back)
    from_inner = [lax.ppermute(piece, "blk", to_inner) for piece in backs]
    total, place = settle(meta, own_sum, adj, sec, from_next)
    return finish(place, total, from_outer, *from_inner)


def solution(mesh):
    placed = (P("blk", None, None, None), P(), P(), P())
    return jax.shard_map(
        per_device, mesh=mesh, in_specs=placed, out_specs=P("blk", None, None), check_vma=False
    )
```

```python
import functools

import jax
import jax.numpy as jnp
from jax import lax
from jax.experimental import pallas as pl
from jax.experimental.pallas import tpu as pltpu
from jax.sharding import PartitionSpec as P

EARLY = 1792
MIB = 1024 * 1024
MAIN_LIMIT, EARLY_LIMIT, LATE_LIMIT = 24 * MIB, 12 * MIB, 12 * MIB
F32 = jnp.float32
BLOCK = 256
TOKEN = pltpu.VMEM((8, 128), jnp.float32)


def dot_rows(left, right):
    return lax.dot_general(left, right, (((1,), (1,)), ((), ())), preferred_element_type=F32)


def flat(block):
    return block.reshape(block.shape[0] * block.shape[1], block.shape[2])


def layout(cap, me, slots_ref):
    even = me % 2 == 0
    start = me // 2 * 4
    odd_live = slots_ref[start + 3] % cap + 1
    live = jnp.where(even, 4 - odd_live, odd_live)
    return live, jnp.where(even, start, start + 4 - odd_live), even


def in_hbm(value):
    return pltpu.with_memory_space_constraint(value, pltpu.HBM)


def run_copies(pairs, sems):
    copies = [pltpu.make_async_copy(source, target, sems.at[n]) for n, (source, target) in enumerate(pairs)]
    for copy in copies:
        copy.start()
    for copy in copies:
        copy.wait()


def pick_kernel(cap, me_ref, slots_ref, own_ref, out_ref, sems):
    live, _, even = layout(cap, me_ref[0], slots_ref)
    slot = jnp.where(even, 0, live - 1)
    width = out_ref.shape[-1]
    run_copies([(own_ref.at[slot, k, :, pl.ds(0, width)], out_ref.at[k]) for k in range(3)], sems)


def pick_two_kernel(cap, start, me_ref, slots_ref, own_ref, partner_ref, after, out_ref, token_ref, sems):
    del after
    token_ref[...] = jnp.zeros_like(token_ref)
    live, _, even = layout(cap, me_ref[0], slots_ref)
    width = out_ref.shape[-1]
    columns = pl.ds(start, width)
    slot = jnp.where(even, 0, live - 1)
    first = [(own_ref.at[slot, k, :, columns], out_ref.at[0, k]) for k in range(3)]

    @pl.when(live >= 2)
    def _():
        second = jnp.where(even, 1, live - 2)
        run_copies(first + [(own_ref.at[second, k, :, columns], out_ref.at[1, k]) for k in range(3)], sems)

    @pl.when(live == 1)
    def _():
        second = jnp.where(even, 0, cap - live)
        run_copies(first + [(partner_ref.at[second, k, :, columns], out_ref.at[1, k]) for k in range(3)], sems)


def pick_call(kernel, name, shape, me, block_slot, blocks, *after):
    smem = pl.BlockSpec(memory_space=pltpu.SMEM)
    moved = 4
    for size in shape:
        moved *= size
    return pl.pallas_call(
        kernel,
        out_shape=(pltpu.VMEM(shape, blocks[0].dtype),) + (TOKEN,) * (len(blocks) - 1),
        in_specs=[smem, smem, pl.BlockSpec(memory_space=pltpu.HBM)]
        + [pl.BlockSpec(memory_space=pl.ANY)] * (len(blocks) - 1 + len(after)),
        out_specs=(pl.BlockSpec(memory_space=pltpu.VMEM),) * len(blocks),
        scratch_shapes=[pltpu.SemaphoreType.DMA((6,))],
        compiler_params=pltpu.CompilerParams(vmem_limit_bytes=LATE_LIMIT),
        name=name,
        cost_estimate=pl.CostEstimate(flops=0, bytes_accessed=moved, transcendentals=0),
    )(me.reshape(1), in_hbm(block_slot), in_hbm(blocks[0]), *blocks[1:], *after)


def pick_early(me, block_slot, own):
    cap, aux, rows, _ = own.shape
    return pick_call(
        functools.partial(pick_kernel, cap), "pick", (aux, rows, EARLY), me, block_slot, [own]
    )[0]


def pick_late(me, block_slot, own, partner, after):
    cap, aux, rows, width = own.shape
    return pick_call(
        functools.partial(pick_two_kernel, cap, EARLY),
        "pick_two",
        (2, aux, rows, width - EARLY),
        me,
        block_slot,
        [own, partner],
        after,
    )


def counts_kernel(cap, me_ref, slots_ref, pairs_ref, domain_ref, counts_ref, meta_ref):
    live, first, even = layout(cap, me_ref[0], slots_ref)
    values = (
        live,
        even.astype(jnp.int32),
        jnp.where(even, 0, live - 1),
        jnp.where(live == 1, 0, jnp.where(even, 1, live - 2)),
        jnp.where(even, live - 1, 0),
        jnp.where(live == 1, 0, jnp.where(even, live - 2, 1)),
        jnp.where(even, 0, cap - live),
    )
    lanes = lax.broadcasted_iota(jnp.int32, meta_ref.shape, 1)
    meta = jnp.zeros(meta_ref.shape, jnp.int32)
    for n, value in enumerate(values):
        meta = jnp.where(lanes == n, value, meta)
    meta_ref[...] = meta
    a = pairs_ref[0:1, :]
    b = pairs_ref[1:2, :]
    edge = (a - (first - 2)) * 2 + (b - a - 1)
    size = a.shape[1]
    rows = lax.broadcasted_iota(jnp.int32, (16, size), 0)
    hot = jnp.where(rows == edge, 1.0, 0.0).astype(jnp.bfloat16)
    weight = jnp.zeros((16, size), F32)
    for j in range(2):
        code = domain_ref[j : j + 1, :] * 3 + domain_ref[j + 2 : j + 3, :]
        weight = weight + jnp.where(rows == code, 1.0, 0.0)
    counts_ref[...] = dot_rows(hot, weight.astype(jnp.bfloat16))


def pair_counts(me, block_slot, pair_list, domain_slots, cap):
    pairs, domain = pair_list.T, domain_slots.T
    vmem = pl.BlockSpec(memory_space=pltpu.VMEM)
    smem = pl.BlockSpec(memory_space=pltpu.SMEM)
    return pl.pallas_call(
        functools.partial(counts_kernel, cap),
        out_shape=(pltpu.VMEM((16, 16), F32), pltpu.VMEM((8, 128), jnp.int32)),
        in_specs=[smem, smem, vmem, vmem],
        out_specs=(vmem, vmem),
        compiler_params=pltpu.CompilerParams(vmem_limit_bytes=LATE_LIMIT),
        name="pair_counts",
        cost_estimate=pl.CostEstimate(flops=4_000_000, bytes_accessed=200_000, transcendentals=0),
    )(me.reshape(1), block_slot, pairs, domain)


def weigh(counts_ref, row, step_left, step_right, left, right_of, total_ref):
    rows = left.shape[0] // 3

    for l in range(3):
        product = dot_rows(left, right_of(l))
        total = total_ref[...]
        for k in range(3):
            count = counts_ref[row, k * step_left + l * step_right]
            total = total + count * product[k * rows : (k + 1) * rows]
        total_ref[...] = total


def split(counts_ref, row, step_own, step_halo, aux_of, l):
    total = None
    for k in range(3):
        part = counts_ref[row, k * step_own + l * step_halo] * aux_of(k).astype(F32)
        total = part if total is None else total + part
    high = total.astype(jnp.bfloat16)
    return high, (total - high.astype(F32)).astype(jnp.bfloat16)


def fill(counts_ref, row, step_own, step_halo, source, store):
    rows = BLOCK

    def one(n, carry):
        l, r = n // (rows // 32), pl.multiple_of(n % (rows // 32) * 32, 32)
        high, low = split(counts_ref, row, step_own, step_halo, lambda k: source(k, r), l)
        store(l, r, high)
        store(l, rows + r, low)
        return carry

    lax.fori_loop(0, 3 * rows // 32, one, 0)


def store_columns(early, early_ref, late_ref):
    def store(l, r, values):
        early_ref[l, pl.ds(r, 32)] = values[:, :early]
        late_ref[l, pl.ds(r, 32)] = values[:, early:]

    return store


def edge_kernel(meta_ref, counts_ref, own_hbm, mix_early, mix_late, mix_far, own_ref, sem):
    live, even = meta_ref[0, 0], meta_ref[0, 1] == 1
    copy = pltpu.make_async_copy(own_hbm.at[meta_ref[0, 2]], own_ref, sem)
    copy.start()
    step_own = jnp.where(even, 1, 3)
    step_halo = jnp.where(even, 3, 1)
    early = mix_early.shape[-1]
    copy.wait()

    def far_store(l, r, values):
        mix_far[l, pl.ds(r, 32)] = values

    row_adj = jnp.where(even, 2, live * 2 + 2)
    row_far = jnp.where(even, 1, live * 2 + 3)
    store = store_columns(early, mix_early, mix_late)
    fill(counts_ref, row_adj, step_own, step_halo, lambda k, r: own_ref[k, pl.ds(r, 32)], store)
    fill(counts_ref, row_far, step_own, step_halo, lambda k, r: own_ref[k, pl.ds(r, 32), early:], far_store)


def edge_part(meta, counts, own):
    cap, aux, rows, width = own.shape
    late = width - EARLY
    smem = pl.BlockSpec(memory_space=pltpu.SMEM)
    vmem = pl.BlockSpec(memory_space=pltpu.VMEM)
    return pl.pallas_call(
        edge_kernel,
        in_specs=[smem, smem, pl.BlockSpec(memory_space=pltpu.HBM)],
        out_specs=(vmem,) * 3,
        scratch_shapes=[pltpu.VMEM((aux, rows, width), own.dtype), pltpu.SemaphoreType.DMA(())],
        out_shape=tuple(pltpu.VMEM((aux, 2 * rows, size), own.dtype) for size in (EARLY, late, late)),
        compiler_params=pltpu.CompilerParams(vmem_limit_bytes=EARLY_LIMIT),
        name="edge_mix",
        cost_estimate=pl.CostEstimate(flops=30_000_000, bytes_accessed=10_000_000, transcendentals=0),
    )(meta, counts, in_hbm(own))


def main_kernel(
    meta_ref, counts_ref, own_hbm, partner_hbm, after, sum_ref, near_ref, next_ref, mix_early, mix_late,
    own_ref, inner_ref, edge_ref, sems
):
    del after
    live, even = meta_ref[0, 0], meta_ref[0, 1] == 1
    sec_out, adjacent, second = meta_ref[0, 3], meta_ref[0, 4], meta_ref[0, 5]
    step_own = jnp.where(even, 3, 1)
    step_halo = jnp.where(even, 1, 3)
    _, _, rows, width = own_ref.shape

    def own_copy(s):
        return pltpu.make_async_copy(own_hbm.at[s], own_ref.at[s], sems.at[s])

    inner_copy = pltpu.make_async_copy(partner_hbm.at[meta_ref[0, 6]], inner_ref.at[0], sems.at[3])
    second_copy = pltpu.make_async_copy(partner_hbm.at[1], inner_ref.at[1], sems.at[4])
    for s in range(3):
        pl.when(s < live)(own_copy(s).start)
        if s == 0:
            pl.when(live < 3)(inner_copy.start)
            pl.when(live == 1)(second_copy.start)
    near_ref[...] = jnp.zeros_like(near_ref)
    next_ref[...] = jnp.zeros_like(next_ref)

    def diag(s, carry):
        @pl.when(s < live)
        def _():
            own_copy(s).wait()
            total = dot_rows(own_ref[s, 0], own_ref[s, 0])
            for k in range(1, 3):
                total = total + dot_rows(own_ref[s, k], own_ref[s, k])
            sum_ref[s] = total

        @pl.when(s >= live)
        def _():
            sum_ref[s] = jnp.zeros((rows, rows), F32)

        return carry

    lax.fori_loop(0, 3, diag, 0)

    def own_edge(e, carry):
        i, j = e // 2, jnp.minimum(e + 1, 2)
        theirs = (live == 3) & (e == jnp.where(even, 2, 0))

        @pl.when((j < live) & jnp.logical_not(theirs))
        def _():
            row = (i + 2) * 2 + (j - i - 1)
            edge_ref[...] = jnp.zeros_like(edge_ref)
            weigh(counts_ref, row, 3, 1, flat(own_ref[i]), lambda l: own_ref[j, l], edge_ref)
            sum_ref[i] += edge_ref[...]
            sum_ref[j] += edge_ref[...].T

        return carry

    lax.fori_loop(0, 3, own_edge, 0)
    pl.when(live < 3)(inner_copy.wait)
    pl.when(live == 1)(second_copy.wait)
    half = width // 2

    def inner_edge(t, carry):
        e, side = t // 2, t % 2
        mine = (live == 1) | ((live == 2) & ((e == 1) | (side == jnp.where(even, 0, 1))))

        @pl.when(mine)
        def _():
            slot = jnp.where(e == 0, adjacent, second)
            halo = jnp.where((live == 1) & (e == 1), 1, 0)
            row_one = jnp.where(live == 1, jnp.where(even, 5, 1), jnp.where(even, live * 2 + 1, 3))
            row = jnp.where(e == 0, jnp.where(even, live * 2 + 2, 2), row_one)
            columns = pl.ds(pl.multiple_of(side * half, half), half)
            edge_ref[...] = jnp.zeros_like(edge_ref)
            weigh(
                counts_ref,
                row,
                step_own,
                step_halo,
                flat(own_ref[slot, :, :, columns]),
                lambda l: inner_ref[halo, l, :, columns],
                edge_ref,
            )
            sum_ref[slot] += edge_ref[...]

            @pl.when(halo == 0)
            def _():
                near_ref[...] += edge_ref[...].T

            @pl.when(halo == 1)
            def _():
                next_ref[...] += edge_ref[...].T


        return carry

    lax.fori_loop(0, 4, inner_edge, 0)

    @pl.when(live == 1)
    def _():
        row = jnp.where(even, 6, 0)
        edge_ref[...] = jnp.zeros_like(edge_ref)
        weigh(counts_ref, row, step_own, step_halo, flat(inner_ref[0]), lambda l: inner_ref[1, l], edge_ref)
        near_ref[...] += edge_ref[...]
        next_ref[...] += edge_ref[...].T

    early = mix_early.shape[-1]

    def put(source):
        row = jnp.where(even, 3, live * 2 + 1)
        fill(counts_ref, row, step_halo, step_own, source, store_columns(early, mix_early, mix_late))

    pl.when(live >= 2)(lambda: put(lambda k, r: own_ref[sec_out, k, pl.ds(r, 32)]))
    pl.when(live == 1)(lambda: put(lambda k, r: inner_ref[0, k, pl.ds(r, 32)]))


def main_part(meta, counts, own, partner, after):
    cap, aux, rows, width = own.shape
    late = width - EARLY
    smem = pl.BlockSpec(memory_space=pltpu.SMEM)
    vmem = pl.BlockSpec(memory_space=pltpu.VMEM)
    hbm = pl.BlockSpec(memory_space=pltpu.HBM)
    free = pl.BlockSpec(memory_space=pl.ANY)
    return pl.pallas_call(
        main_kernel,
        in_specs=[smem, smem, hbm, free, free],
        out_specs=(vmem,) * 5,
        scratch_shapes=[
            pltpu.VMEM((cap, aux, rows, width), own.dtype),
            pltpu.VMEM((2, aux, rows, width), own.dtype),
            pltpu.VMEM((rows, rows), F32),
            pltpu.SemaphoreType.DMA((5,)),
        ],
        out_shape=(
            jax.ShapeDtypeStruct((cap, rows, rows), F32),
            jax.ShapeDtypeStruct((rows, rows), F32),
            jax.ShapeDtypeStruct((rows, rows), F32),
            pltpu.VMEM((aux, 2 * rows, EARLY), own.dtype),
            pltpu.VMEM((aux, 2 * rows, late), own.dtype),
        ),
        compiler_params=pltpu.CompilerParams(vmem_limit_bytes=MAIN_LIMIT),
        name="own_and_inner",
        cost_estimate=pl.CostEstimate(
            flops=50 * 2 * rows * rows * width, bytes_accessed=16_000_000, transcendentals=0
        ),
    )(meta, counts, in_hbm(own), partner, after)


def mixed(mix_ref, right_of):
    total = None
    for l in range(3):
        part = dot_rows(mix_ref[l], right_of(l))
        total = part if total is None else total + part
    rows = total.shape[1]
    return total[:rows] + total[rows:]


def early_kernel(mix_ref, outer_ref, back_ref, sec_ref):
    sec = mixed(mix_ref, lambda l: outer_ref[l])
    back_ref[...] = sec.T
    sec_ref[...] = sec


def early_part(mix, outer):
    aux, rows, width = outer.shape
    vmem = pl.BlockSpec(memory_space=pltpu.VMEM)
    return pl.pallas_call(
        early_kernel,
        in_specs=[vmem] * 2,
        out_specs=(vmem,) * 2,
        out_shape=(jax.ShapeDtypeStruct((rows, rows), F32),) * 2,
        compiler_params=pltpu.CompilerParams(vmem_limit_bytes=EARLY_LIMIT),
        name="outer_early",
        cost_estimate=pl.CostEstimate(
            flops=6 * 2 * rows * rows * width, bytes_accessed=1_000_000, transcendentals=0
        ),
    )(mix, outer)


def adjacent_kernel(mix_ref, outer_ref, adj_ref):
    adj_ref[...] = mixed(mix_ref, lambda l: outer_ref[l])


def adjacent_part(mix, outer):
    aux, rows, width = outer.shape
    vmem = pl.BlockSpec(memory_space=pltpu.VMEM)
    return pl.pallas_call(
        adjacent_kernel,
        in_specs=[vmem] * 2,
        out_specs=vmem,
        out_shape=jax.ShapeDtypeStruct((rows, rows), F32),
        compiler_params=pltpu.CompilerParams(vmem_limit_bytes=EARLY_LIMIT),
        name="outer_adjacent",
        cost_estimate=pl.CostEstimate(
            flops=6 * 2 * rows * rows * width, bytes_accessed=1_000_000, transcendentals=0
        ),
    )(mix, outer)


def late_kernel(
    meta_ref, adj_mix, sec_mix, far_mix, outer_ref, adj_in, sec_in, inner_in, adj_ref, sec_ref, *inner_refs
):
    sec = sec_in[...] + mixed(sec_mix, lambda l: outer_ref[0, l])
    adj = mixed(adj_mix, lambda l: outer_ref[0, l]) + mixed(far_mix, lambda l: outer_ref[1, l])
    near = inner_in[...] + jnp.where(meta_ref[0, 0] == 1, sec, 0.0)
    half = near.shape[0] // 2
    inner_refs[0][...] = near[:half]
    inner_refs[1][...] = near[half:]
    sec_ref[...] = sec
    adj_ref[...] = adj_in[...] + adj


def late_part(meta, mixes, outer, adj, sec, inner_back):
    _, aux, rows, width = outer.shape
    square = jax.ShapeDtypeStruct((rows, rows), F32)
    vmem = pl.BlockSpec(memory_space=pltpu.VMEM)
    return pl.pallas_call(
        late_kernel,
        in_specs=[pl.BlockSpec(memory_space=pltpu.SMEM)] + [vmem] * 7,
        out_specs=(vmem,) * 4,
        out_shape=(square, square) + (jax.ShapeDtypeStruct((rows // 2, rows), F32),) * 2,
        compiler_params=pltpu.CompilerParams(vmem_limit_bytes=LATE_LIMIT),
        name="outer_late",
        cost_estimate=pl.CostEstimate(
            flops=18 * 2 * rows * rows * width, bytes_accessed=1_000_000, transcendentals=0
        ),
    )(meta, *mixes, outer, adj, sec, inner_back)


def settle_kernel(meta_ref, sum_ref, adj_ref, sec_ref, next_ref, out_ref, place_ref):
    out_ref[...] = sum_ref[...]
    out_ref[meta_ref[0, 5]] += next_ref[...]
    out_ref[meta_ref[0, 2]] += adj_ref[...]

    @pl.when(meta_ref[0, 0] >= 2)
    def _():
        out_ref[meta_ref[0, 3]] += sec_ref[...]

    row = lax.broadcasted_iota(jnp.int32, place_ref.shape, 0)
    hit = (row == meta_ref[0, 2]) | (row == meta_ref[0, 4] + 3)
    place_ref[...] = jnp.where(hit, 1.0, 0.0)


def settle(meta, total, *blocks):
    vmem = pl.BlockSpec(memory_space=pltpu.VMEM)
    return pl.pallas_call(
        settle_kernel,
        in_specs=[pl.BlockSpec(memory_space=pltpu.SMEM)] + [vmem] * (1 + len(blocks)),
        out_specs=(vmem, vmem),
        out_shape=(pltpu.VMEM(total.shape, F32), pltpu.VMEM((8, total.shape[2]), F32)),
        compiler_params=pltpu.CompilerParams(vmem_limit_bytes=LATE_LIMIT),
        name="settle",
        cost_estimate=pl.CostEstimate(flops=200_000, bytes_accessed=2_000_000, transcendentals=0),
    )(meta, total, *blocks)


def finish_kernel(place_ref, sum_ref, outer_ref, near_top, near_low, out_ref):
    half = near_top.shape[0]
    for s in range(3):
        for rows, near in ((slice(0, half), near_top), (slice(half, 2 * half), near_low)):
            out_ref[s, rows] = (
                sum_ref[s, rows]
                + place_ref[s : s + 1] * outer_ref[rows]
                + place_ref[3 + s : 4 + s] * near[...]
            )


def finish(place, total, *blocks):
    vmem = pl.BlockSpec(memory_space=pltpu.VMEM)
    return pl.pallas_call(
        finish_kernel,
        in_specs=[vmem] * (2 + len(blocks)),
        out_specs=vmem,
        out_shape=jax.ShapeDtypeStruct(total.shape, F32),
        compiler_params=pltpu.CompilerParams(vmem_limit_bytes=LATE_LIMIT),
        name="finish",
        cost_estimate=pl.CostEstimate(flops=200_000, bytes_accessed=2_000_000, transcendentals=0),
    )(place, total, *blocks)


def per_device(own, block_slot, pair_list, domain_slots):
    cap = own.shape[0]
    count = lax.axis_size("blk")
    me = lax.axis_index("blk")
    to_outer = [(d, d - 1) for d in range(2, count, 2)] + [(d, d + 1) for d in range(1, count - 1, 2)]
    to_inner = [(d, d ^ 1) for d in range(count)]
    outer_early = lax.ppermute(pick_early(me, block_slot, own), "blk", to_outer)
    partner = lax.ppermute(own, "blk", to_inner)
    counts, meta = pair_counts(me, block_slot, pair_list, domain_slots, cap)
    adj_early, adj_late, mix_far = edge_part(meta, counts, own)
    late_piece, token = pick_late(me, block_slot, own, partner, mix_far)
    outer_late = lax.ppermute(late_piece, "blk", to_outer)
    own_sum, inner_back, next_back, sec_early, sec_late = main_part(meta, counts, own, partner, token)
    from_next = lax.ppermute(next_back, "blk", to_inner)
    outer_back, sec = early_part(sec_early, outer_early)
    from_outer = lax.ppermute(outer_back, "blk", to_outer)
    adj = adjacent_part(adj_early, outer_early)
    adj, sec, *backs = late_part(meta, (adj_late, sec_late, mix_far), outer_late, adj, sec, inner_back)
    from_inner = [lax.ppermute(piece, "blk", to_inner) for piece in backs]
    total, place = settle(meta, own_sum, adj, sec, from_next)
    return finish(place, total, from_outer, *from_inner)


def solution(mesh):
    placed = (P("blk", None, None, None), P(), P(), P())
    return jax.shard_map(
        per_device, mesh=mesh, in_specs=placed, out_specs=P("blk", None, None), check_vma=False
    )
```
